512 devices in a mesh: tok: 64 (over y, z_lo, core), slab: 8 (over z_hi, x).
Axes of the slice: x: 4, y: 4, z: 16 (z_hi: 2, z_lo: 8; z = z_hi * 8 + z_lo), core: 2. Of those that a mesh axis runs over, the one named last changes fastest.
Arguments:
- activations: bfloat16 [32768, 32, 256], P('tok', 'slab'), may hold values from -40 to 40, as said below
- block_map: int32 [8, 16, 2], P('slab'), may hold values from -1 to 31, as said below
Outputs:
- hessian_blocks: float32 [8, 4096, 256], P('slab', 'tok')
The draws below stay inside these ranges and needn't reach their ends.
Inputs may be any that keep to these rules, and one draw needn't show every extreme that they name: `block_map`: each slot holds either (i, j) with 0 <= i <= j < 32 and j among slab s's blocks s * 4 to s * 4 + 3, or (-1, -1) for an empty slot; empty slots come after the live ones; no block appears twice; the last slab has all 16 slots live. `activations`: values of order one.
All inputs are finite; a program needn't handle non-finite values.
Results may differ from the reference program's by a relative error of at most 0.0003.
Values may be sent and summed in bfloat16 or wider, within the bound.
No kernel may reach another device: no remote copies, remote signals or barrier semaphores. Data moves between devices by JAX's collectives and lax.ppermute only.
A program may use at most 64 MiB of HBM per device.

```python
import math
import jax
import jax.numpy as jnp
from jax import lax

BLOCK = 256
NB = 32
CB = 4
TOKENS = 32768
MOST = 16
N_SLAB = 8


def draw_activations(key, part):
    key = jax.random.fold_in(key, 11)
    keys = jax.random.split(key, 4)
    noise = jax.random.normal(keys[0], (TOKENS, NB, BLOCK), jnp.float32)
    common = jax.random.normal(keys[1], (TOKENS, 1, 8), jnp.float32)
    weight = 0.5
    row_scale = jnp.exp(jax.random.uniform(keys[2], (TOKENS, 1, 1), jnp.float32, math.log(0.5), math.log(2.0)))
    col_scale = jnp.exp(jax.random.uniform(keys[3], (1, NB, BLOCK), jnp.float32, -0.5 * math.log(10.0), 0.5 * math.log(10.0)))
    shared = jnp.tile(common, (1, NB, BLOCK // 8))
    values = (noise + weight * shared) * row_scale * col_scale
    return jnp.clip(values, -40.0, 40.0).astype(jnp.bfloat16)


def draw_block_map(key, part):
    key = jax.random.fold_in(key, 23)
    candidates = jnp.arange(NB * CB, dtype=jnp.int32)
    row_of = candidates // CB
    local_col = candidates % CB

    def one_slab(slab_key, slab_id):
        col_of = slab_id * CB + local_col
        valid = (row_of <= col_of).astype(jnp.int32)
        order = jax.random.permutation(jax.random.fold_in(slab_key, 1), NB * CB).astype(jnp.int32)
        scores = order + valid * (NB * CB)
        picked = lax.top_k(scores, MOST)[1]
        total = jnp.sum(valid)
        wanted = jax.random.randint(jax.random.fold_in(slab_key, 2), (), MOST // 4, MOST + 1)
        wanted = jnp.where(slab_id == N_SLAB - 1, MOST, wanted)
        count = jnp.minimum(wanted, total)
        keep = jnp.arange(MOST, dtype=jnp.int32) < count
        rows = jnp.where(keep, row_of[picked], -1)
        cols = jnp.where(keep, col_of[picked], -1)
        return jnp.stack([rows, cols], axis=1).astype(jnp.int32)
    slab_keys = jax.random.split(key, N_SLAB)
    return jax.vmap(one_slab)(slab_keys, jnp.arange(N_SLAB, dtype=jnp.int32))


def setup_inputs(seed: int = 0) -> dict:
    seeds = jax.random.split(jax.random.key(seed), 3)
    activations = draw_activations(jax.random.fold_in(seeds[2], 71), 0)
    block_map = draw_block_map(jax.random.fold_in(seeds[2], 71), 0)
    return {"activations": activations, "block_map": block_map}


def reference(activations, block_map):
    slots = block_map.reshape(N_SLAB * MOST, 2)

    def one_block(pair):
        row_index = jnp.maximum(pair[0], 0).astype(jnp.int32)
        col_index = jnp.maximum(pair[1], 0).astype(jnp.int32)
        left = lax.dynamic_index_in_dim(activations, row_index, 1, keepdims=False)
        right = lax.dynamic_index_in_dim(activations, col_index, 1, keepdims=False)
        product = jnp.dot(left.T, right, preferred_element_type=jnp.float32)
        live = (pair[0] >= 0).astype(jnp.float32)
        return product * live * (2.0 / TOKENS)

    blocks = lax.map(one_block, slots)
    return blocks.reshape(N_SLAB, MOST * BLOCK, BLOCK)
```

```python
import jax
import jax.numpy as jnp
from jax import lax
from jax.experimental import pallas as pl
from jax.experimental.pallas import tpu as pltpu
from jax.sharding import Mesh, PartitionSpec as P

NY, NZ, NC, NH, NX = 4, 8, 2, 2, 4
WAVES = 2


def shift_x(v, d, upper_only=False):
    halves = (1,) if upper_only else (0, 1)
    pairs = [(h * NX + i, h * NX + (i - d) % NX) for h in halves for i in range(NX)]
    return lax.ppermute(v, ("zh", "x"), pairs)


def products_kernel(meta, *refs):
    n = 4 + 4 * WAVES
    sources, (keep, send, rows, row_sems, own, own_sem) = refs[:n], refs[n:]
    slots = rows.shape[0]
    y, zl, core = meta[0], meta[1], meta[2]
    own_copy = pltpu.make_async_copy(sources[0], own, own_sem)
    own_copy.start()

    def fetch(k, _):
        for b in range(n):

            @pl.when(meta[8 + k] == b)
            def _():
                pltpu.make_async_copy(
                    sources[b].at[meta[24 + k]], rows.at[k], row_sems.at[k]
                ).start()

        return 0

    lax.fori_loop(0, slots, fetch, 0)
    own_copy.wait()

    def one(k, _):
        pltpu.make_async_copy(sources[0].at[0], rows.at[k], row_sems.at[k]).wait()
        product = lax.dot_general(
            rows[k],
            own[meta[40 + k]],
            (((0,), (0,)), ((), ())),
            preferred_element_type=jnp.float32,
        )
        product = jnp.where(meta[56 + k] > 0, product, 0.0)
        group = lax.rem(k // 4 - y + NY, NY)
        for half in range(2):
            e = (lax.rem(k, 4) * 2 + half) ^ zl
            place = ((e & 1) << 2) | (e & 2) | (e >> 2)
            at = pl.ds(pl.multiple_of((group * 8 + place) * 64, 64), 64)
            first = product[half * 128 : half * 128 + 64]
            second = product[half * 128 + 64 : half * 128 + 128]
            keep[at, :] = jnp.where(core == 0, first, second)
            send[at, :] = jnp.where(core == 0, second, first)
        return 0

    lax.fori_loop(0, slots, one, 0)


def products(meta, sources, slots, tokens, width):
    half = slots * width // 2
    return pl.pallas_call(
        products_kernel,
        out_shape=[jax.ShapeDtypeStruct((half, width), jnp.float32)] * 2,
        in_specs=[pl.BlockSpec(memory_space=pltpu.SMEM)]
        + [pl.BlockSpec(memory_space=pl.ANY)] * len(sources),
        out_specs=[pl.BlockSpec(memory_space=pltpu.VMEM)] * 2,
        scratch_shapes=[
            pltpu.VMEM((slots, tokens, width), jnp.bfloat16),
            pltpu.SemaphoreType.DMA((slots,)),
            pltpu.VMEM((4, tokens, width), jnp.bfloat16),
            pltpu.SemaphoreType.DMA,
        ],
        compiler_params=pltpu.CompilerParams(vmem_limit_bytes=24 << 20),
        cost_estimate=pl.CostEstimate(
            flops=2 * slots * tokens * width * width,
            bytes_accessed=12 << 20,
            transcendentals=0,
        ),
    )(meta, *sources)


def body(activations, block_map):
    tokens, blocks, width = activations.shape
    y, zl, core = (lax.axis_index(a) for a in ("y", "zl", "core"))
    zh, x = lax.axis_index("zh"), lax.axis_index("x")
    slots = block_map[0]
    count = slots.shape[0]
    row, col = slots[:, 0], slots[:, 1]
    live = row >= 0
    slab, place = jnp.maximum(row, 0) // blocks, jnp.maximum(row, 0) % blocks
    step = (slab - x) % NX
    same = slab // NX == zh
    per = blocks // WAVES
    buffer = jnp.where(live, jnp.where(same, step, 4 + place // per * 4 + step), 0)
    inside = jnp.where(live, jnp.where(same, place, place % per), 0)
    local = jnp.where(live, col - (zh * NX + x) * blocks, 0)
    where = jnp.stack([y, zl, core, zh, x, zh, zh, zh]).astype(jnp.int32)
    meta = jnp.concatenate([where, buffer, inside, local, live.astype(jnp.int32)])

    own = jnp.transpose(activations, (1, 0, 2))
    waves = []
    for w in range(WAVES):
        waves.append(lax.ppermute(own[w * per : w * per + per], "zh", [(0, 1)]))
    sources = [own] + [shift_x(own, d) for d in (1, 2, 3)]
    for low in waves:
        sources += [low] + [shift_x(low, d, True) for d in (1, 2, 3)]

    keep, send = products(meta, sources, count, tokens, width)
    total = keep + lax.ppermute(send, "core", [(0, 1), (1, 0)])
    part = total.shape[0] // NY
    mine = total[:part]
    for d in (1, 2, 3):
        mine = mine + lax.ppermute(
            total[d * part : d * part + part], "y", [(i, (i + d) % NY) for i in range(NY)]
        )
    for bit in (1, 2, 4):
        half = mine.shape[0] // 2
        mine = mine[:half] + lax.ppermute(mine[half:], "zl", [(i, i ^ bit) for i in range(NZ)])
    scale = 2.0 / (tokens * NY * NZ * NC)
    return (mine * scale)[None]


def solution(mesh):
    grid = Mesh(mesh.devices.reshape(NY, NZ, NC, NH, NX), ("y", "zl", "core", "zh", "x"))
    tok, slab = ("y", "zl", "core"), ("zh", "x")
    return jax.shard_map(
        body,
        mesh=grid,
        in_specs=(P(tok, slab, None), P(slab, None, None)),
        out_specs=P(slab, tok, None),
        check_vma=False,
    )
```

```python
import functools

import jax
import jax.numpy as jnp
from jax import lax
from jax.experimental import pallas as pl
from jax.experimental.pallas import tpu as pltpu
from jax.sharding import Mesh, PartitionSpec as P

NY, NZ, NC, NH, NX = 4, 8, 2, 2, 4
SIZES = {"y": NY, "zl": NZ, "core": NC, "x": NX}
QUARTER = 64
VMEM = pl.BlockSpec(memory_space=pltpu.VMEM)
SMEM = pl.BlockSpec(memory_space=pltpu.SMEM)
ANY = pl.BlockSpec(memory_space=pl.ANY)


def swap(v, axis, e):
    return lax.ppermute(v, axis, [(i, i ^ e) for i in range(SIZES[axis])])


def quarter_picker(x, width):
    p = lax.broadcasted_iota(jnp.int32, (QUARTER, width), 0)
    f = lax.broadcasted_iota(jnp.int32, (QUARTER, width), 1)
    wanted = (p // 32) * 128 + ((p // 16) % 2) * 64 + x * 16 + p % 16
    return (f == wanted).astype(jnp.float32).astype(jnp.bfloat16)


def pick(picker, block):
    return lax.dot_general(
        picker, block, (((1,), (1,)), ((), ())), preferred_element_type=jnp.float32
    ).astype(jnp.bfloat16)


def quarters_kernel(meta, pairs, own, load, *outs):
    blocks, tokens, width = own.shape
    for d in range(NX):
        picker = quarter_picker(meta[0] ^ d, width)
        for b in range(blocks):
            outs[d][b] = pick(picker, own[b])
    for b in range(blocks):
        load[b * tokens : (b + 1) * tokens] = own[b]
    slots = pairs.shape[0]
    slot = lax.broadcasted_iota(jnp.int32, (slots, width), 0)
    lane = lax.broadcasted_iota(jnp.int32, (slots, width), 1)
    table = jnp.zeros((slots, width), jnp.int32)
    for k in range(slots):
        table = jnp.where(slot == k, jnp.where(lane == 0, pairs[k, 0], pairs[k, 1]), table)
    load[blocks * tokens :] = table.astype(jnp.float32).astype(jnp.bfloat16)


def quarters(x, pairs, own):
    blocks, tokens, width = own.shape
    rows = blocks * tokens + pairs.shape[0]
    return pl.pallas_call(
        quarters_kernel,
        out_shape=[jax.ShapeDtypeStruct((rows, width), jnp.bfloat16)]
        + [jax.ShapeDtypeStruct((blocks, QUARTER, tokens), jnp.bfloat16)] * NX,
        in_specs=[SMEM, SMEM, VMEM],
        out_specs=[VMEM] * (1 + NX),
        compiler_params=pltpu.CompilerParams(vmem_limit_bytes=16 << 20),
    )(x[None].astype(jnp.int32), pairs, own)


HEAD = 8


def put(meta, n, product, keep, send):
    y, zl, core, x = meta[0], meta[1], meta[2], meta[3]
    k = lax.rem(n, 16)
    group = (k // 4) ^ y
    for half in range(2):
        e = (lax.rem(k, 4) * 2 + half) ^ zl
        place = ((e & 1) << 2) | (e & 2) | (e >> 2)
        at = pl.ds(pl.multiple_of(((group * 8 + place) * NX + (n // 16 ^ x)) * 16, 16), 16)
        if product is None:
            keep[at, :] = jnp.zeros((16, keep.shape[1]), jnp.float32)
            send[at, :] = jnp.zeros((16, keep.shape[1]), jnp.float32)
        else:
            first = product[half * 32 : half * 32 + 16]
            second = product[half * 32 + 16 : half * 32 + 32]
            keep[at, :] = jnp.where(core == 0, first, second)
            send[at, :] = jnp.where(core == 0, second, first)


def early_kernel(slots, meta, source, keep, send, cols, rows, sems):
    tokens = cols.shape[1]
    per = cols.shape[0] // NX
    copies = [
        pltpu.make_async_copy(source.at[b // per, pl.ds(b % per * tokens, tokens)], cols.at[b], sems.at[b])
        for b in range(cols.shape[0])
    ]
    for copy in copies:
        copy.start()
    picker = quarter_picker(meta[3], cols.shape[2])
    for b, copy in enumerate(copies):
        copy.wait()
        rows[b] = pick(picker, cols[b])

    def one(n, _):
        @pl.when(meta[HEAD + n] == 0)
        def _():
            put(meta, n, None, keep, send)

        @pl.when(meta[HEAD + n] == 1)
        def _():
            product = jnp.dot(
                rows[meta[HEAD + slots + n]],
                cols[meta[HEAD + 2 * slots + n]],
                preferred_element_type=jnp.float32,
            )
            put(meta, n, product, keep, send)

        return 0

    lax.fori_loop(0, slots, one, 0)


def late_kernel(slots, meta, cols, *refs):
    sources, (_, _, keep, send, rows, sems) = refs[:NX], refs[NX:]
    per = sources[0].shape[0]
    copies = [
        pltpu.make_async_copy(sources[d], rows.at[pl.ds(d * per, per)], sems.at[d])
        for d in range(NX)
    ]
    for copy in copies:
        copy.start()
    for copy in copies:
        copy.wait()

    def one(n, _):
        @pl.when(meta[HEAD + n] == 2)
        def _():
            product = jnp.dot(
                rows[meta[HEAD + slots + n]],
                cols[meta[HEAD + 2 * slots + n]],
                preferred_element_type=jnp.float32,
            )
            put(meta, n, product, keep, send)

        return 0

    lax.fori_loop(0, slots, one, 0)


def early(meta, source, count, tokens, slots):
    width = source.shape[2]
    half = jax.ShapeDtypeStruct((slots * QUARTER // 2, width), jnp.float32)
    return pl.pallas_call(
        functools.partial(early_kernel, slots),
        out_shape=[half, half, jax.ShapeDtypeStruct((count, tokens, width), jnp.bfloat16)],
        in_specs=[SMEM, ANY],
        out_specs=[VMEM] * 3,
        scratch_shapes=[
            pltpu.VMEM((count, QUARTER, tokens), jnp.bfloat16),
            pltpu.SemaphoreType.DMA((count,)),
        ],
        compiler_params=pltpu.CompilerParams(vmem_limit_bytes=24 << 20),
    )(meta, source)


def late(meta, cols, sources, keep, send, slots):
    per, quarter, tokens = sources[0].shape
    half = jax.ShapeDtypeStruct(keep.shape, jnp.float32)
    return pl.pallas_call(
        functools.partial(late_kernel, slots),
        out_shape=[half, half],
        in_specs=[SMEM, VMEM] + [ANY] * NX + [VMEM] * 2,
        out_specs=[VMEM] * 2,
        scratch_shapes=[
            pltpu.VMEM((NX * per, quarter, tokens), jnp.bfloat16),
            pltpu.SemaphoreType.DMA((NX,)),
        ],
        input_output_aliases={2 + NX: 0, 3 + NX: 1},
        compiler_params=pltpu.CompilerParams(vmem_limit_bytes=24 << 20),
    )(meta, cols, *sources, keep, send)


def body(activations, block_map):
    tokens, blocks, width = activations.shape
    y, zl, core = (lax.axis_index(a) for a in ("y", "zl", "core"))
    zh, x = lax.axis_index("zh"), lax.axis_index("x")

    own = jnp.transpose(activations, (1, 0, 2))
    load, *pieces = quarters(x, block_map[0], own)
    low = [
        lax.ppermute(piece, ("zh", "x"), [(i, NX + (i ^ e)) for i in range(NX)])
        for e, piece in enumerate(pieces)
    ]
    half = lax.all_to_all(jnp.broadcast_to(load, (NX, *load.shape)), "x", 0, 0, tiled=True)
    pairs = half[:, blocks * tokens :, :2].astype(jnp.int32).reshape(-1, 2)
    slots = pairs.shape[0]
    row, col = jnp.maximum(pairs[:, 0], 0), jnp.maximum(pairs[:, 1], 0)
    live, same = pairs[:, 0] >= 0, row // blocks // NX == zh
    kind = jnp.where(live, jnp.where(same, 1, 2), 0)
    row_at = jnp.where(same, row // blocks % NX, row // blocks % NX ^ x) * blocks + row % blocks
    col_at = col % (NX * blocks)
    head = jnp.stack([y, zl, core, x, zh, zh, zh, zh])
    meta = jnp.concatenate([head, kind, row_at, col_at]).astype(jnp.int32)

    keep, send, cols = early(meta, half, NX * blocks, tokens, slots)
    keep, send = late(meta, cols, low, keep, send, slots)

    total = keep + swap(send, "core", 1)
    part = total.shape[0] // NY
    mine = total[:part]
    for e in (2, 1, 3):
        mine = mine + swap(total[e * part : e * part + part], "y", e)
    for bit in (1, 2, 4):
        half = mine.shape[0] // 2
        mine = mine[:half] + swap(mine[half:], "zl", bit)
    mine = mine * (2.0 / (tokens * NY * NZ * NC))
    part = mine.shape[0] // NX
    a = [mine[:part]] + [swap(mine[e * part : e * part + part], "x", e) for e in (1, 2, 3)]
    odd, high = x % 2 == 1, x >= 2
    a = [jnp.where(odd, a[q ^ 1], a[q]) for q in range(NX)]
    a = [jnp.where(high, a[q ^ 2], a[q]) for q in range(NX)]
    return jnp.concatenate(a)[None]


def solution(mesh):
    grid = Mesh(mesh.devices.reshape(NY, NZ, NC, NH, NX), ("y", "zl", "core", "zh", "x"))
    tok, slab = ("y", "zl", "core"), ("zh", "x")
    return jax.shard_map(
        body,
        mesh=grid,
        in_specs=(P(tok, slab, None), P(slab, None, None)),
        out_specs=P(slab, tok, None),
        check_vma=False,
    )
```

```python
import functools

import jax
import jax.numpy as jnp
from jax import lax
from jax.experimental import pallas as pl
from jax.experimental.pallas import tpu as pltpu
from jax.sharding import Mesh, PartitionSpec as P

NY, NZ, NC, NH, NX = 4, 8, 2, 2, 4
SIZES = {"y": NY, "zl": NZ, "core": NC, "x": NX}
CUTS = 2
QUARTER = 64
VMEM = pl.BlockSpec(memory_space=pltpu.VMEM)
SMEM = pl.BlockSpec(memory_space=pltpu.SMEM)
ANY = pl.BlockSpec(memory_space=pl.ANY)


def swap(v, axis, e):
    return lax.ppermute(v, axis, [(i, i ^ e) for i in range(SIZES[axis])])


def quarter_picker(x, width):
    p = lax.broadcasted_iota(jnp.int32, (QUARTER, width), 0)
    f = lax.broadcasted_iota(jnp.int32, (QUARTER, width), 1)
    wanted = (p // 32) * 128 + ((p // 16) % 2) * 64 + x * 16 + p % 16
    return (f == wanted).astype(jnp.float32).astype(jnp.bfloat16)


def pick(picker, block):
    return lax.dot_general(
        picker, block, (((1,), (1,)), ((), ())), preferred_element_type=jnp.float32
    ).astype(jnp.bfloat16)


def quarters_kernel(meta, pairs, own, load, *outs):
    blocks, tokens, width = own.shape
    for d in range(NX):
        picker = quarter_picker(meta[0] ^ d, width)
        for b in range(blocks):
            outs[d][b] = pick(picker, own[b])
    slots = pairs.shape[0]
    slot = lax.broadcasted_iota(jnp.int32, (slots, width), 0)
    lane = lax.broadcasted_iota(jnp.int32, (slots, width), 1)
    table = jnp.zeros((slots, width), jnp.int32)
    for k in range(slots):
        table = jnp.where(slot == k, jnp.where(lane == 0, pairs[k, 0], pairs[k, 1]), table)
    table = table.astype(jnp.float32).astype(jnp.bfloat16)
    for d in range(NX):
        for b in range(blocks):
            load[d, b * tokens : (b + 1) * tokens] = own[b]
        load[d, blocks * tokens :] = table


def quarters(x, pairs, own):
    blocks, tokens, width = own.shape
    rows = blocks * tokens + pairs.shape[0]
    return pl.pallas_call(
        quarters_kernel,
        out_shape=[jax.ShapeDtypeStruct((NX, rows, width), jnp.bfloat16)]
        + [jax.ShapeDtypeStruct((blocks, QUARTER, tokens), jnp.bfloat16)] * NX,
        in_specs=[SMEM, SMEM, VMEM],
        out_specs=[VMEM] * (1 + NX),
        compiler_params=pltpu.CompilerParams(vmem_limit_bytes=16 << 20),
    )(x[None].astype(jnp.int32), pairs, own)


HEAD = 8


def put(meta, n, product, keep, send):
    y, core = meta[0], meta[2]
    k = lax.rem(n, 16)
    e = k // 4 ^ y
    groups = [e ^ (e >> 1), ((e ^ (e >> 1)) >> 1) | ((e & 1) ^ (e >> 1)) << 1]
    for half in range(2):
        place = lax.rem(k, 4) * 2 + half
        for cut in range(CUTS):
            at = pl.ds(pl.multiple_of(((groups[cut] * 8 + place) * NX + n // 16) * 16, 16), 16)
            wide = keep[cut].shape[1]
            lanes = slice(cut * wide, (cut + 1) * wide)
            if product is None:
                keep[cut][at, :] = jnp.zeros((16, wide), jnp.float32)
                send[cut][at, :] = jnp.zeros((16, wide), jnp.float32)
            else:
                first = product[half * 32 : half * 32 + 16, lanes]
                second = product[half * 32 + 16 : half * 32 + 32, lanes]
                keep[cut][at, :] = jnp.where(core == 0, first, second)
                send[cut][at, :] = jnp.where(core == 0, second, first)


def early_kernel(slots, meta, source, *refs):
    keep, send, (cols, rows, sems) = refs[:CUTS], refs[CUTS : 2 * CUTS], refs[2 * CUTS :]
    tokens = cols.shape[1]
    per = cols.shape[0] // NX
    copies = [
        pltpu.make_async_copy(source.at[b // per, pl.ds(b % per * tokens, tokens)], cols.at[b], sems.at[b])
        for b in range(cols.shape[0])
    ]
    for copy in copies:
        copy.start()
    picker = quarter_picker(meta[3], cols.shape[2])
    for b, copy in enumerate(copies):
        copy.wait()
        rows[b] = pick(picker, cols[b])

    def one(n, _):
        @pl.when(meta[HEAD + n] == 0)
        def _():
            put(meta, n, None, keep, send)

        @pl.when(meta[HEAD + n] == 1)
        def _():
            product = jnp.dot(
                rows[meta[HEAD + slots + n]],
                cols[meta[HEAD + 2 * slots + n]],
                preferred_element_type=jnp.float32,
            )
            put(meta, n, product, keep, send)

        return 0

    lax.fori_loop(0, slots, one, 0)


def late_kernel(slots, meta, cols, *refs):
    sources, refs = refs[:NX], refs[NX + 2 * CUTS :]
    keep, send, (rows, sems) = refs[:CUTS], refs[CUTS : 2 * CUTS], refs[2 * CUTS :]
    per = sources[0].shape[0]
    copies = [
        pltpu.make_async_copy(sources[d], rows.at[pl.ds(d * per, per)], sems.at[d])
        for d in range(NX)
    ]
    for copy in copies:
        copy.start()
    for copy in copies:
        copy.wait()

    def one(n, _):
        @pl.when(meta[HEAD + n] == 2)
        def _():
            product = jnp.dot(
                rows[meta[HEAD + slots + n]],
                cols[meta[HEAD + 2 * slots + n]],
                preferred_element_type=jnp.float32,
            )
            put(meta, n, product, keep, send)

        return 0

    lax.fori_loop(0, slots, one, 0)


def early(meta, source, count, tokens, slots):
    width = source.shape[2]
    half = jax.ShapeDtypeStruct((slots * QUARTER // 2, width // CUTS), jnp.float32)
    return pl.pallas_call(
        functools.partial(early_kernel, slots),
        out_shape=[half] * (2 * CUTS) + [jax.ShapeDtypeStruct((count, tokens, width), jnp.bfloat16)],
        in_specs=[SMEM, ANY],
        out_specs=[VMEM] * (2 * CUTS + 1),
        scratch_shapes=[
            pltpu.VMEM((count, QUARTER, tokens), jnp.bfloat16),
            pltpu.SemaphoreType.DMA((count,)),
        ],
        compiler_params=pltpu.CompilerParams(vmem_limit_bytes=24 << 20),
    )(meta, source)


def late(meta, cols, sources, halves, slots):
    per, quarter, tokens = sources[0].shape
    return pl.pallas_call(
        functools.partial(late_kernel, slots),
        out_shape=[jax.ShapeDtypeStruct(h.shape, h.dtype) for h in halves],
        in_specs=[SMEM, VMEM] + [ANY] * NX + [VMEM] * len(halves),
        out_specs=[VMEM] * len(halves),
        scratch_shapes=[
            pltpu.VMEM((NX * per, quarter, tokens), jnp.bfloat16),
            pltpu.SemaphoreType.DMA((NX,)),
        ],
        input_output_aliases={2 + NX + i: i for i in range(len(halves))},
        compiler_params=pltpu.CompilerParams(vmem_limit_bytes=24 << 20),
    )(meta, cols, *sources, *halves)


def body(activations, block_map):
    tokens, blocks, width = activations.shape
    y, zl, core = (lax.axis_index(a) for a in ("y", "zl", "core"))
    zh, x = lax.axis_index("zh"), lax.axis_index("x")

    own = jnp.transpose(activations, (1, 0, 2))
    load, *pieces = quarters(x, block_map[0], own)
    low = [
        lax.ppermute(piece, ("zh", "x"), [(i, NX + (i ^ e)) for i in range(NX)])
        for e, piece in enumerate(pieces)
    ]
    half = lax.all_to_all(load, "x", 0, 0, tiled=True)
    pairs = half[:, blocks * tokens :, :2].astype(jnp.int32).reshape(-1, 2)
    slots = pairs.shape[0]
    row, col = jnp.maximum(pairs[:, 0], 0), jnp.maximum(pairs[:, 1], 0)
    live, same = pairs[:, 0] >= 0, row // blocks // NX == zh
    kind = jnp.where(live, jnp.where(same, 1, 2), 0)
    row_at = jnp.where(same, row // blocks % NX, row // blocks % NX ^ x) * blocks + row % blocks
    col_at = col % (NX * blocks)
    head = jnp.stack([y, zl, core, x, zh, zh, zh, zh])
    meta = jnp.concatenate([head, kind, row_at, col_at]).astype(jnp.int32)

    *halves, cols = early(meta, half, NX * blocks, tokens, slots)
    halves = late(meta, cols, low, halves, slots)
    scale = 2.0 / (tokens * NY * NZ * NC)
    cuts = [total(keep, send, order) for keep, send, order in zip(halves[:CUTS], halves[CUTS:], ((3, 1), (1, 3)))]
    parts = jnp.concatenate(cuts, axis=1).reshape(NZ * NX, -1, width)
    parts = lax.all_to_all(parts, ("zl", "x"), 0, 0, tiled=True).reshape(NZ, -1, width)
    return jnp.sum(parts, axis=0)[None] * scale


def total(keep, send, order):
    kept = keep + swap(send, "core", 1)
    for e in order:
        half = kept.shape[0] // 2
        kept = kept[:half] + swap(kept[half:], "y", e)
    return kept


def solution(mesh):
    grid = Mesh(mesh.devices.reshape(NY, NZ, NC, NH, NX), ("y", "zl", "core", "zh", "x"))
    tok, slab = ("y", "zl", "core"), ("zh", "x")
    return jax.shard_map(
        body,
        mesh=grid,
        in_specs=(P(tok, slab, None), P(slab, None, None)),
        out_specs=P(slab, tok, None),
        check_vma=False,
    )
```

```python
import functools

import jax
import jax.numpy as jnp
from jax import lax
from jax.experimental import pallas as pl
from jax.experimental.pallas import tpu as pltpu
from jax.sharding import Mesh, PartitionSpec as P

NY, NZ, NC, NH, NX = 4, 8, 2, 2, 4
SIZES = {"y": NY, "zl": NZ, "core": NC, "x": NX}
CUTS = 2
QUARTER = 64
VMEM = pl.BlockSpec(memory_space=pltpu.VMEM)
SMEM = pl.BlockSpec(memory_space=pltpu.SMEM)
ANY = pl.BlockSpec(memory_space=pl.ANY)


def swap(v, axis, e):
    return lax.ppermute(v, axis, [(i, i ^ e) for i in range(SIZES[axis])])


def quarter_picker(x, width):
    p = lax.broadcasted_iota(jnp.int32, (QUARTER, width), 0)
    f = lax.broadcasted_iota(jnp.int32, (QUARTER, width), 1)
    wanted = (p // 32) * 128 + ((p // 16) % 2) * 64 + x * 16 + p % 16
    return (f == wanted).astype(jnp.float32).astype(jnp.bfloat16)


def pick(picker, block):
    return lax.dot_general(
        picker, block, (((1,), (1,)), ((), ())), preferred_element_type=jnp.float32
    ).astype(jnp.bfloat16)


def quarters_kernel(meta, own, *outs):
    for d in range(NX):
        picker = quarter_picker(meta[0] ^ d, own.shape[2])
        for b in range(own.shape[0]):
            outs[d][b] = pick(picker, own[b])


def quarters(x, own):
    blocks, tokens, width = own.shape
    return pl.pallas_call(
        quarters_kernel,
        out_shape=[jax.ShapeDtypeStruct((blocks, QUARTER, tokens), jnp.bfloat16)] * NX,
        in_specs=[SMEM, VMEM],
        out_specs=[VMEM] * NX,
        compiler_params=pltpu.CompilerParams(vmem_limit_bytes=16 << 20),
    )(x[None].astype(jnp.int32), own)


def exchange(own, pairs):
    blocks, tokens, width = own.shape
    table = jnp.pad(pairs.astype(jnp.bfloat16), ((0, 0), (0, width - pairs.shape[1])))
    load = jnp.concatenate([own.reshape(blocks * tokens, width), table])
    return lax.all_to_all(jnp.broadcast_to(load, (NX, *load.shape)), "x", 0, 0, tiled=True)


HEAD = 8


def put(meta, n, product, keep, send):
    y, core = meta[0], meta[2]
    k = lax.rem(n, 16)
    e = k // 4 ^ y
    groups = [e ^ (e >> 1), ((e ^ (e >> 1)) >> 1) | ((e & 1) ^ (e >> 1)) << 1]
    for half in range(2):
        place = lax.rem(k, 4) * 2 + half
        for cut in range(CUTS):
            at = pl.ds(pl.multiple_of(((groups[cut] * 8 + place) * NX + n // 16) * 16, 16), 16)
            wide = keep[cut].shape[1]
            lanes = slice(cut * wide, (cut + 1) * wide)
            if product is None:
                keep[cut][at, :] = jnp.zeros((16, wide), jnp.float32)
                send[cut][at, :] = jnp.zeros((16, wide), jnp.float32)
            else:
                first = product[half * 32 : half * 32 + 16, lanes]
                second = product[half * 32 + 16 : half * 32 + 32, lanes]
                keep[cut][at, :] = jnp.where(core == 0, first, second)
                send[cut][at, :] = jnp.where(core == 0, second, first)


def early_kernel(slots, meta, source, *refs):
    keep, send, (cols, rows, sems) = refs[:CUTS], refs[CUTS : 2 * CUTS], refs[2 * CUTS :]
    tokens = cols.shape[1]
    per = cols.shape[0] // NX
    copies = [
        pltpu.make_async_copy(source.at[b // per, pl.ds(b % per * tokens, tokens)], cols.at[b], sems.at[b])
        for b in range(cols.shape[0])
    ]
    for copy in copies:
        copy.start()
    picker = quarter_picker(meta[3], cols.shape[2])
    for b, copy in enumerate(copies):
        copy.wait()
        rows[b] = pick(picker, cols[b])

    def one(n, _):
        @pl.when(meta[HEAD + n] == 0)
        def _():
            put(meta, n, None, keep, send)

        @pl.when(meta[HEAD + n] == 1)
        def _():
            product = jnp.dot(
                rows[meta[HEAD + slots + n]],
                cols[meta[HEAD + 2 * slots + n]],
                preferred_element_type=jnp.float32,
            )
            put(meta, n, product, keep, send)

        return 0

    lax.fori_loop(0, slots, one, 0)


def late_kernel(slots, meta, cols, *refs):
    sources, refs = refs[:NX], refs[NX + 2 * CUTS :]
    keep, send, (rows, sems) = refs[:CUTS], refs[CUTS : 2 * CUTS], refs[2 * CUTS :]
    per = sources[0].shape[0]
    copies = [
        pltpu.make_async_copy(sources[d], rows.at[pl.ds(d * per, per)], sems.at[d])
        for d in range(NX)
    ]
    for copy in copies:
        copy.start()
    for copy in copies:
        copy.wait()

    def one(n, _):
        @pl.when(meta[HEAD + n] == 2)
        def _():
            product = jnp.dot(
                rows[meta[HEAD + slots + n]],
                cols[meta[HEAD + 2 * slots + n]],
                preferred_element_type=jnp.float32,
            )
            put(meta, n, product, keep, send)

        return 0

    lax.fori_loop(0, slots, one, 0)


def early(meta, source, count, tokens, slots):
    width = source.shape[2]
    half = jax.ShapeDtypeStruct((slots * QUARTER // 2, width // CUTS), jnp.float32)
    return pl.pallas_call(
        functools.partial(early_kernel, slots),
        out_shape=[half] * (2 * CUTS) + [jax.ShapeDtypeStruct((count, tokens, width), jnp.bfloat16)],
        in_specs=[SMEM, ANY],
        out_specs=[VMEM] * (2 * CUTS + 1),
        scratch_shapes=[
            pltpu.VMEM((count, QUARTER, tokens), jnp.bfloat16),
            pltpu.SemaphoreType.DMA((count,)),
        ],
        compiler_params=pltpu.CompilerParams(vmem_limit_bytes=24 << 20),
        cost_estimate=pl.CostEstimate(flops=0, bytes_accessed=0, transcendentals=0),
    )(meta, source)


def late(meta, cols, sources, halves, slots):
    per, quarter, tokens = sources[0].shape
    return pl.pallas_call(
        functools.partial(late_kernel, slots),
        out_shape=[jax.ShapeDtypeStruct(h.shape, h.dtype) for h in halves],
        in_specs=[SMEM, VMEM] + [ANY] * NX + [VMEM] * len(halves),
        out_specs=[VMEM] * len(halves),
        scratch_shapes=[
            pltpu.VMEM((NX * per, quarter, tokens), jnp.bfloat16),
            pltpu.SemaphoreType.DMA((NX,)),
        ],
        input_output_aliases={2 + NX + i: i for i in range(len(halves))},
        compiler_params=pltpu.CompilerParams(vmem_limit_bytes=24 << 20),
    )(meta, cols, *sources, *halves)


def body(activations, block_map):
    tokens, blocks, width = activations.shape
    y, zl, core = (lax.axis_index(a) for a in ("y", "zl", "core"))
    zh, x = lax.axis_index("zh"), lax.axis_index("x")

    own = jnp.transpose(activations, (1, 0, 2))
    pieces = quarters(x, own)
    low = [
        lax.ppermute(piece, ("zh", "x"), [(i, NX + (i ^ e)) for i in range(NX)])
        for e, piece in enumerate(pieces)
    ]
    rows = blocks * tokens + block_map.shape[1]
    half = lax.cond(
        block_map[0, 0, 0] >= -1,
        exchange,
        lambda own, pairs: jnp.zeros((NX, rows, width), own.dtype),
        own,
        block_map[0],
    )
    pairs = half[:, blocks * tokens :, :2].astype(jnp.int32).reshape(-1, 2)
    slots = pairs.shape[0]
    row, col = jnp.maximum(pairs[:, 0], 0), jnp.maximum(pairs[:, 1], 0)
    live, same = pairs[:, 0] >= 0, row // blocks // NX == zh
    kind = jnp.where(live, jnp.where(same, 1, 2), 0)
    row_at = jnp.where(same, row // blocks % NX, row // blocks % NX ^ x) * blocks + row % blocks
    col_at = col % (NX * blocks)
    head = jnp.stack([y, zl, core, x, zh, zh, zh, zh])
    meta = jnp.concatenate([head, kind, row_at, col_at]).astype(jnp.int32)

    *halves, cols = early(meta, half, NX * blocks, tokens, slots)
    halves = late(meta, cols, low, halves, slots)
    scale = 2.0 / (tokens * NY * NZ * NC)
    cuts = [total(keep, send, order) for keep, send, order in zip(halves[:CUTS], halves[CUTS:], ((3, 1), (1, 3)))]
    parts = jnp.concatenate(cuts, axis=1).reshape(NZ * NX, -1, width)
    parts = lax.all_to_all(parts, ("zl", "x"), 0, 0, tiled=True).reshape(NZ, -1, width)
    return jnp.sum(parts, axis=0)[None] * scale


def total(keep, send, order):
    kept = keep + swap(send, "core", 1)
    for e in order:
        half = kept.shape[0] // 2
        kept = kept[:half] + swap(kept[half:], "y", e)
    return kept


def solution(mesh):
    grid = Mesh(mesh.devices.reshape(NY, NZ, NC, NH, NX), ("y", "zl", "core", "zh", "x"))
    tok, slab = ("y", "zl", "core"), ("zh", "x")
    return jax.shard_map(
        body,
        mesh=grid,
        in_specs=(P(tok, slab, None), P(slab, None, None)),
        out_specs=P(slab, tok, None),
        check_vma=False,
    )
```

```python
import functools

import jax
import jax.numpy as jnp
from jax import lax
from jax.experimental import pallas as pl
from jax.experimental.pallas import tpu as pltpu
from jax.sharding import Mesh, PartitionSpec as P

NY, NZ, NC, NH, NX = 4, 8, 2, 2, 4
NP = NZ // 2
SIZES = {"y": NY, "zi": 2, "core": NC, "x": NX}
CUTS = 2
QUARTER = 64
VMEM = pl.BlockSpec(memory_space=pltpu.VMEM)
SMEM = pl.BlockSpec(memory_space=pltpu.SMEM)
ANY = pl.BlockSpec(memory_space=pl.ANY)


def swap(v, axis, e):
    return lax.ppermute(v, axis, [(i, i ^ e) for i in range(SIZES[axis])])


def quarter_picker(x, width):
    p = lax.broadcasted_iota(jnp.int32, (QUARTER, width), 0)
    f = lax.broadcasted_iota(jnp.int32, (QUARTER, width), 1)
    wanted = (p // 32) * 128 + ((p // 16) % 2) * 64 + x * 16 + p % 16
    return (f == wanted).astype(jnp.float32).astype(jnp.bfloat16)


def pick(picker, block):
    return lax.dot_general(
        picker, block, (((1,), (1,)), ((), ())), preferred_element_type=jnp.float32
    ).astype(jnp.bfloat16)


def quarters_kernel(meta, own, *outs):
    for d in range(NX):
        picker = quarter_picker(meta[0] ^ d, own.shape[2])
        for b in range(own.shape[0]):
            outs[d][b] = pick(picker, own[b])


def quarters(x, own):
    blocks, tokens, width = own.shape
    return pl.pallas_call(
        quarters_kernel,
        out_shape=[jax.ShapeDtypeStruct((blocks, QUARTER, tokens), jnp.bfloat16)] * NX,
        in_specs=[SMEM, VMEM],
        out_specs=[VMEM] * NX,
        compiler_params=pltpu.CompilerParams(vmem_limit_bytes=16 << 20),
    )(x[None].astype(jnp.int32), own)


def exchange(own, pairs):
    blocks, tokens, width = own.shape
    table = jnp.pad(pairs.astype(jnp.bfloat16), ((0, 0), (0, width - pairs.shape[1])))
    load = jnp.concatenate([own.reshape(blocks * tokens, width), table])
    return lax.all_to_all(jnp.broadcast_to(load, (NX, *load.shape)), "x", 0, 0, tiled=True)


HEAD = 8


def put(meta, n, product, keep, send):
    y, zi, core = meta[0], meta[1], meta[2]
    k = lax.rem(n, 16)
    e = k // 4 ^ y
    group = e ^ (e >> 1)
    for half in range(2):
        side = half ^ zi
        starts = (group * 2 + side, side * 4 + group)
        for cut in range(CUTS):
            at = ((starts[cut] * NP + lax.rem(k, 4)) * NX + n // 16) * 16
            at = pl.ds(pl.multiple_of(at, 16), 16)
            wide = keep[cut].shape[1]
            lanes = slice(cut * wide, (cut + 1) * wide)
            if product is None:
                keep[cut][at, :] = jnp.zeros((16, wide), jnp.float32)
                send[cut][at, :] = jnp.zeros((16, wide), jnp.float32)
            else:
                first = product[half * 32 : half * 32 + 16, lanes]
                second = product[half * 32 + 16 : half * 32 + 32, lanes]
                keep[cut][at, :] = jnp.where(core == 0, first, second)
                send[cut][at, :] = jnp.where(core == 0, second, first)


def early_kernel(slots, meta, source, *refs):
    keep, send, (cols, rows, sems) = refs[:CUTS], refs[CUTS : 2 * CUTS], refs[2 * CUTS :]
    tokens = cols.shape[1]
    per = cols.shape[0] // NX
    copies = [
        pltpu.make_async_copy(source.at[b // per, pl.ds(b % per * tokens, tokens)], cols.at[b], sems.at[b])
        for b in range(cols.shape[0])
    ]
    for copy in copies:
        copy.start()
    picker = quarter_picker(meta[3], cols.shape[2])
    for b, copy in enumerate(copies):
        copy.wait()
        rows[b] = pick(picker, cols[b])

    def one(n, _):
        @pl.when(meta[HEAD + n] == 0)
        def _():
            put(meta, n, None, keep, send)

        @pl.when(meta[HEAD + n] == 1)
        def _():
            product = jnp.dot(
                rows[meta[HEAD + slots + n]],
                cols[meta[HEAD + 2 * slots + n]],
                preferred_element_type=jnp.float32,
            )
            put(meta, n, product, keep, send)

        return 0

    lax.fori_loop(0, slots, one, 0)


def late_kernel(slots, meta, cols, *refs):
    sources, refs = refs[:NX], refs[NX + 2 * CUTS :]
    keep, send, (rows, sems) = refs[:CUTS], refs[CUTS : 2 * CUTS], refs[2 * CUTS :]
    per = sources[0].shape[0]
    copies = [
        pltpu.make_async_copy(sources[d], rows.at[pl.ds(d * per, per)], sems.at[d])
        for d in range(NX)
    ]
    for copy in copies:
        copy.start()
    for copy in copies:
        copy.wait()

    def one(n, _):
        @pl.when(meta[HEAD + n] == 2)
        def _():
            product = jnp.dot(
                rows[meta[HEAD + slots + n]],
                cols[meta[HEAD + 2 * slots + n]],
                preferred_element_type=jnp.float32,
            )
            put(meta, n, product, keep, send)

        return 0

    lax.fori_loop(0, slots, one, 0)


def early(meta, source, count, tokens, slots):
    width = source.shape[2]
    half = jax.ShapeDtypeStruct((slots * QUARTER // 2, width // CUTS), jnp.float32)
    return pl.pallas_call(
        functools.partial(early_kernel, slots),
        out_shape=[half] * (2 * CUTS) + [jax.ShapeDtypeStruct((count, tokens, width), jnp.bfloat16)],
        in_specs=[SMEM, ANY],
        out_specs=[VMEM] * (2 * CUTS + 1),
        scratch_shapes=[
            pltpu.VMEM((count, QUARTER, tokens), jnp.bfloat16),
            pltpu.SemaphoreType.DMA((count,)),
        ],
        compiler_params=pltpu.CompilerParams(vmem_limit_bytes=24 << 20),
        cost_estimate=pl.CostEstimate(flops=0, bytes_accessed=0, transcendentals=0),
    )(meta, source)


def late(meta, cols, sources, halves, slots):
    per, quarter, tokens = sources[0].shape
    return pl.pallas_call(
        functools.partial(late_kernel, slots),
        out_shape=[jax.ShapeDtypeStruct(h.shape, h.dtype) for h in halves],
        in_specs=[SMEM, VMEM] + [ANY] * NX + [VMEM] * len(halves),
        out_specs=[VMEM] * len(halves),
        scratch_shapes=[
            pltpu.VMEM((NX * per, quarter, tokens), jnp.bfloat16),
            pltpu.SemaphoreType.DMA((NX,)),
        ],
        input_output_aliases={2 + NX + i: i for i in range(len(halves))},
        compiler_params=pltpu.CompilerParams(vmem_limit_bytes=24 << 20),
    )(meta, cols, *sources, *halves)


def body(activations, block_map):
    tokens, blocks, width = activations.shape
    y, zi, core = (lax.axis_index(a) for a in ("y", "zi", "core"))
    zh, x = lax.axis_index("zh"), lax.axis_index("x")

    own = jnp.transpose(activations, (1, 0, 2))
    pieces = quarters(x, own)
    low = [
        lax.ppermute(piece, ("zh", "x"), [(i, NX + (i ^ e)) for i in range(NX)])
        for e, piece in enumerate(pieces)
    ]
    rows = blocks * tokens + block_map.shape[1]
    half = lax.cond(
        block_map[0, 0, 0] >= -1,
        exchange,
        lambda own, pairs: jnp.zeros((NX, rows, width), own.dtype),
        own,
        block_map[0],
    )
    pairs = half[:, blocks * tokens :, :2].astype(jnp.int32).reshape(-1, 2)
    slots = pairs.shape[0]
    row, col = jnp.maximum(pairs[:, 0], 0), jnp.maximum(pairs[:, 1], 0)
    live, same = pairs[:, 0] >= 0, row // blocks // NX == zh
    kind = jnp.where(live, jnp.where(same, 1, 2), 0)
    row_at = jnp.where(same, row // blocks % NX, row // blocks % NX ^ x) * blocks + row % blocks
    col_at = col % (NX * blocks)
    head = jnp.stack([y, zi, core, x, zh, zh, zh, zh])
    meta = jnp.concatenate([head, kind, row_at, col_at]).astype(jnp.int32)

    *halves, cols = early(meta, half, NX * blocks, tokens, slots)
    halves = late(meta, cols, low, halves, slots)
    scale = 2.0 / (tokens * NY * NZ * NC)
    orders = ((("y", 3), ("y", 1), ("zi", 1)), (("zi", 1), ("y", 3), ("y", 1)))
    cuts = [total(*cut) for cut in zip(halves[:CUTS], halves[CUTS:], orders)]
    parts = jnp.concatenate(cuts, axis=1).reshape(NP * NX, -1, width)
    parts = lax.all_to_all(parts, ("zp", "x"), 0, 0, tiled=True).reshape(NP, -1, width)
    return jnp.sum(parts, axis=0)[None] * scale


def total(keep, send, order):
    kept = keep + swap(send, "core", 1)
    for axis, e in order:
        half = kept.shape[0] // 2
        kept = kept[:half] + swap(kept[half:], axis, e)
    return kept


def solution(mesh):
    grid = mesh.devices.reshape(NY, NP, 2, NC, NH, NX)
    tok, slab = ("y", "zp", "zi", "core"), ("zh", "x")
    return jax.shard_map(
        body,
        mesh=Mesh(grid, tok + slab),
        in_specs=(P(tok, slab, None), P(slab, None, None)),
        out_specs=P(slab, tok, None),
        check_vma=False,
    )
```

```python
import functools

import jax
import jax.numpy as jnp
from jax import lax
from jax.experimental import pallas as pl
from jax.experimental.pallas import tpu as pltpu
from jax.sharding import Mesh, PartitionSpec as P

NY, NZ, NC, NH, NX = 4, 8, 2, 2, 4
NP = NZ // 2
SIZES = {"y": NY, "zi": 2, "core": NC, "x": NX}
CUTS = 2
TOGETHER = 4
LIST = TOGETHER
QUARTER = 64
VMEM = pl.BlockSpec(memory_space=pltpu.VMEM)
SMEM = pl.BlockSpec(memory_space=pltpu.SMEM)
ANY = pl.BlockSpec(memory_space=pl.ANY)


def swap(v, axis, e):
    return lax.ppermute(v, axis, [(i, i ^ e) for i in range(SIZES[axis])])


def quarter_picker(x, width):
    p = lax.broadcasted_iota(jnp.int32, (QUARTER, width), 0)
    f = lax.broadcasted_iota(jnp.int32, (QUARTER, width), 1)
    wanted = (p // 32) * 128 + ((p // 16) % 2) * 64 + x * 16 + p % 16
    return (f == wanted).astype(jnp.float32).astype(jnp.bfloat16)


def pick(picker, block):
    return lax.dot_general(
        picker, block, (((1,), (1,)), ((), ())), preferred_element_type=jnp.float32
    ).astype(jnp.bfloat16)


def quarters_kernel(meta, own, *outs):
    for d in range(NX):
        picker = quarter_picker(meta[0] ^ d, own.shape[2])
        for b in range(own.shape[0]):
            outs[d][b] = pick(picker, own[b])


def quarters(x, own):
    blocks, tokens, width = own.shape
    return pl.pallas_call(
        quarters_kernel,
        out_shape=[jax.ShapeDtypeStruct((blocks, QUARTER, tokens), jnp.bfloat16)] * NX,
        in_specs=[SMEM, VMEM],
        out_specs=[VMEM] * NX,
        compiler_params=pltpu.CompilerParams(vmem_limit_bytes=16 << 20),
    )(x[None].astype(jnp.int32), own)


def exchange(own, pairs):
    blocks, tokens, width = own.shape
    table = jnp.pad(pairs.astype(jnp.bfloat16), ((0, 0), (0, width - pairs.shape[1])))
    load = jnp.concatenate([own.reshape(blocks * tokens, width), table])
    return lax.all_to_all(jnp.broadcast_to(load, (NX, *load.shape)), "x", 0, 0, tiled=True)


HEAD = 8


def put(meta, n, product, keep, send):
    y, zi, core = meta[0], meta[1], meta[2]
    k = lax.rem(n, 16)
    e = k // 4 ^ y
    group = e ^ (e >> 1)
    for half in range(2):
        side = half ^ zi
        starts = (side * 4 + group, group * 2 + side)
        for cut in range(CUTS):
            at = ((starts[cut] * NP + lax.rem(k, 4)) * NX + n // 16) * 16
            at = pl.ds(pl.multiple_of(at, 16), 16)
            wide = keep[cut].shape[1]
            lanes = slice(cut * wide, (cut + 1) * wide)
            if product is None:
                keep[cut][at, :] = jnp.zeros((16, wide), jnp.float32)
                send[cut][at, :] = jnp.zeros((16, wide), jnp.float32)
            else:
                first = product[half * 32 : half * 32 + 16, lanes]
                second = product[half * 32 + 16 : half * 32 + 32, lanes]
                keep[cut][at, :] = jnp.where(core == 0, first, second)
                send[cut][at, :] = jnp.where(core == 0, second, first)


def early_kernel(slots, meta, source, *refs):
    keep, send, (cols, lists, rows, sems) = refs[:CUTS], refs[CUTS : 2 * CUTS], refs[2 * CUTS :]
    tokens = cols.shape[1]
    per = cols.shape[0] // NX
    copies = [
        pltpu.make_async_copy(source.at[b // per, pl.ds(b % per * tokens, tokens)], cols.at[b], sems.at[b])
        for b in range(cols.shape[0])
    ]
    for copy in copies:
        copy.start()
    picker = quarter_picker(meta[3], cols.shape[2])
    for b, copy in enumerate(copies):
        copy.wait()
        rows[b] = pick(picker, cols[b])

    def one(n, _):
        @pl.when(meta[HEAD + n] == 0)
        def _():
            put(meta, n, None, keep, send)

        @pl.when(meta[HEAD + n] == 1)
        def _():
            product = jnp.dot(
                rows[meta[HEAD + slots + n]],
                cols[meta[HEAD + 2 * slots + n]],
                preferred_element_type=jnp.float32,
            )
            put(meta, n, product, keep, send)

        return 0

    lax.fori_loop(0, slots, one, 0)

    stride = LIST + slots
    for e in range(NX):
        lists[e * stride] = 0

    def note(n, _):
        @pl.when(meta[HEAD + n] == 2)
        def _():
            at = meta[HEAD + slots + n] // (cols.shape[0] // NX) * stride
            count = lists[at] + 1
            lists[at] = count
            for u in range(LIST):
                lists[at + count + u] = n

        return 0

    lax.fori_loop(0, slots, note, 0)


def late_kernel(slots, meta, lists, cols, *refs):
    sources, refs = refs[:NX], refs[NX + 2 * CUTS :]
    keep, send, (rows, sems) = refs[:CUTS], refs[CUTS : 2 * CUTS], refs[2 * CUTS :]
    per = sources[0].shape[0]
    copies = [
        pltpu.make_async_copy(sources[e], rows.at[pl.ds(e * per, per)], sems.at[e])
        for e in range(NX)
    ]
    for copy in copies:
        copy.start()
    for e in range(NX):
        copies[e].wait()

        def some(i, _):
            ids = [lists[e * (LIST + slots) + 1 + i * TOGETHER + u] for u in range(TOGETHER)]
            made = [
                jnp.dot(
                    rows[meta[HEAD + slots + n]],
                    cols[meta[HEAD + 2 * slots + n]],
                    preferred_element_type=jnp.float32,
                )
                for n in ids
            ]
            for n, product in zip(ids, made):
                put(meta, n, product, keep, send)
            return 0

        lax.fori_loop(0, (lists[e * (LIST + slots)] + TOGETHER - 1) // TOGETHER, some, 0)


def early(meta, source, count, tokens, slots):
    width = source.shape[2]
    half = jax.ShapeDtypeStruct((slots * QUARTER // 2, width // CUTS), jnp.float32)
    return pl.pallas_call(
        functools.partial(early_kernel, slots),
        out_shape=[half] * (2 * CUTS)
        + [
            jax.ShapeDtypeStruct((count, tokens, width), jnp.bfloat16),
            jax.ShapeDtypeStruct((NX * (LIST + slots),), jnp.int32),
        ],
        in_specs=[SMEM, ANY],
        out_specs=[VMEM] * (2 * CUTS + 1) + [SMEM],
        scratch_shapes=[
            pltpu.VMEM((count, QUARTER, tokens), jnp.bfloat16),
            pltpu.SemaphoreType.DMA((count,)),
        ],
        compiler_params=pltpu.CompilerParams(vmem_limit_bytes=24 << 20),
        cost_estimate=pl.CostEstimate(flops=0, bytes_accessed=0, transcendentals=0),
    )(meta, source)


def late(meta, lists, cols, sources, halves, slots):
    per, quarter, tokens = sources[0].shape
    return pl.pallas_call(
        functools.partial(late_kernel, slots),
        out_shape=[jax.ShapeDtypeStruct(h.shape, h.dtype) for h in halves],
        in_specs=[SMEM, SMEM, VMEM] + [ANY] * NX + [VMEM] * len(halves),
        out_specs=[VMEM] * len(halves),
        scratch_shapes=[
            pltpu.VMEM((NX * per, quarter, tokens), jnp.bfloat16),
            pltpu.SemaphoreType.DMA((NX,)),
        ],
        input_output_aliases={3 + NX + i: i for i in range(len(halves))},
        compiler_params=pltpu.CompilerParams(vmem_limit_bytes=24 << 20),
    )(meta, lists, cols, *sources, *halves)


def body(activations, block_map):
    tokens, blocks, width = activations.shape
    y, zi, core = (lax.axis_index(a) for a in ("y", "zi", "core"))
    zh, x = lax.axis_index("zh"), lax.axis_index("x")

    own = jnp.transpose(activations, (1, 0, 2))
    pieces = quarters(x, own)
    low = [
        lax.ppermute(piece, ("zh", "x"), [(i, NX + (i ^ e)) for i in range(NX)])
        for e, piece in enumerate(pieces)
    ]
    rows = blocks * tokens + block_map.shape[1]
    half = lax.cond(
        block_map[0, 0, 0] >= -1,
        exchange,
        lambda own, pairs: jnp.zeros((NX, rows, width), own.dtype),
        own,
        block_map[0],
    )
    pairs = half[:, blocks * tokens :, :2].astype(jnp.int32).reshape(-1, 2)
    slots = pairs.shape[0]
    row, col = jnp.maximum(pairs[:, 0], 0), jnp.maximum(pairs[:, 1], 0)
    live, same = pairs[:, 0] >= 0, row // blocks // NX == zh
    kind = jnp.where(live, jnp.where(same, 1, 2), 0)
    row_at = jnp.where(same, row // blocks % NX, row // blocks % NX ^ x) * blocks + row % blocks
    col_at = col % (NX * blocks)
    head = jnp.stack([y, zi, core, x, zh, zh, zh, zh])
    meta = jnp.concatenate([head, kind, row_at, col_at]).astype(jnp.int32)

    *halves, cols, lists = early(meta, half, NX * blocks, tokens, slots)
    halves = late(meta, lists, cols, low, halves, slots)
    scale = 2.0 / (tokens * NY * NZ * NC)
    orders = ((("zi", 1), ("y", 3), ("y", 1)), (("y", 3), ("y", 1), ("zi", 1)))
    cuts = [total(*cut) for cut in zip(halves[:CUTS], halves[CUTS:], orders)]
    parts = jnp.concatenate(cuts, axis=1).reshape(NP * NX, -1, width)
    parts = lax.all_to_all(parts, ("zp", "x"), 0, 0, tiled=True).reshape(NP, -1, width)
    return jnp.sum(parts, axis=0)[None] * scale


def total(keep, send, order):
    kept = keep + swap(send, "core", 1)
    for axis, e in order:
        half = kept.shape[0] // 2
        kept = kept[:half] + swap(kept[half:], axis, e)
    return kept


def solution(mesh):
    grid = mesh.devices.reshape(NY, NP, 2, NC, NH, NX)
    tok, slab = ("y", "zp", "zi", "core"), ("zh", "x")
    return jax.shard_map(
        body,
        mesh=Mesh(grid, tok + slab),
        in_specs=(P(tok, slab, None), P(slab, None, None)),
        out_specs=P(slab, tok, None),
        check_vma=False,
    )
```

```python
import functools

import jax
import jax.numpy as jnp
from jax import lax
from jax.experimental import pallas as pl
from jax.experimental.pallas import tpu as pltpu
from jax.sharding import Mesh, PartitionSpec as P

NY, NZ, NC, NH, NX = 4, 8, 2, 2, 4
NP = NZ // 2
SIZES = {"y": NY, "zi": 2, "core": NC, "x": NX}
CUTS = 2
TOGETHER = 4
LIST = TOGETHER
QUARTER = 64
VMEM = pl.BlockSpec(memory_space=pltpu.VMEM)
SMEM = pl.BlockSpec(memory_space=pltpu.SMEM)
ANY = pl.BlockSpec(memory_space=pl.ANY)


def swap(v, axis, e):
    return lax.ppermute(v, axis, [(i, i ^ e) for i in range(SIZES[axis])])


def quarter_picker(x, width):
    p = lax.broadcasted_iota(jnp.int32, (QUARTER, width), 0)
    f = lax.broadcasted_iota(jnp.int32, (QUARTER, width), 1)
    wanted = (p // 32) * 128 + ((p // 16) % 2) * 64 + x * 16 + p % 16
    return (f == wanted).astype(jnp.float32).astype(jnp.bfloat16)


def pick(picker, block):
    return lax.dot_general(
        picker, block, (((1,), (1,)), ((), ())), preferred_element_type=jnp.float32
    ).astype(jnp.bfloat16)


def quarters_kernel(meta, own, *outs):
    for d in range(NX):
        picker = quarter_picker(meta[0] ^ d, own.shape[2])
        for b in range(own.shape[0]):
            outs[d][b] = pick(picker, own[b])


def quarters(x, own):
    blocks, tokens, width = own.shape
    return pl.pallas_call(
        quarters_kernel,
        out_shape=[jax.ShapeDtypeStruct((blocks, QUARTER, tokens), jnp.bfloat16)] * NX,
        in_specs=[SMEM, VMEM],
        out_specs=[VMEM] * NX,
        compiler_params=pltpu.CompilerParams(vmem_limit_bytes=16 << 20),
    )(x[None].astype(jnp.int32), own)


def exchange(own, pairs):
    blocks, tokens, width = own.shape
    table = jnp.pad(pairs.astype(jnp.bfloat16), ((0, 0), (0, width - pairs.shape[1])))
    load = jnp.concatenate([own.reshape(blocks * tokens, width), table])
    return lax.all_to_all(jnp.broadcast_to(load, (NX, *load.shape)), "x", 0, 0, tiled=True)


HEAD = 8


def put(meta, n, product, keep, send):
    y, zi, core = meta[0], meta[1], meta[2]
    k = lax.rem(n, 16)
    e = k // 4 ^ y
    group = e ^ (e >> 1)
    for half in range(2):
        side = half ^ zi
        starts = (group * 2 + side, side * 4 + k // 4)
        for cut in range(CUTS):
            at = ((starts[cut] * NP + lax.rem(k, 4)) * NX + n // 16) * 16
            at = pl.ds(pl.multiple_of(at, 16), 16)
            wide = keep[cut].shape[1]
            lanes = slice(cut * wide, (cut + 1) * wide)
            if product is None:
                keep[cut][at, :] = jnp.zeros((16, wide), jnp.float32)
                send[cut][at, :] = jnp.zeros((16, wide), jnp.float32)
            else:
                first = product[half * 32 : half * 32 + 16, lanes]
                second = product[half * 32 + 16 : half * 32 + 32, lanes]
                keep[cut][at, :] = jnp.where(core == 0, first, second)
                send[cut][at, :] = jnp.where(core == 0, second, first)


def early_kernel(slots, meta, source, *refs):
    keep, send, (cols, lists, rows, sems) = refs[:CUTS], refs[CUTS : 2 * CUTS], refs[2 * CUTS :]
    tokens = cols.shape[1]
    per = cols.shape[0] // NX
    copies = [
        pltpu.make_async_copy(source.at[b // per, pl.ds(b % per * tokens, tokens)], cols.at[b], sems.at[b])
        for b in range(cols.shape[0])
    ]
    for copy in copies:
        copy.start()
    picker = quarter_picker(meta[3], cols.shape[2])
    for b, copy in enumerate(copies):
        copy.wait()
        rows[b] = pick(picker, cols[b])

    def one(n, _):
        @pl.when(meta[HEAD + n] == 0)
        def _():
            put(meta, n, None, keep, send)

        @pl.when(meta[HEAD + n] == 1)
        def _():
            product = jnp.dot(
                rows[meta[HEAD + slots + n]],
                cols[meta[HEAD + 2 * slots + n]],
                preferred_element_type=jnp.float32,
            )
            put(meta, n, product, keep, send)

        return 0

    lax.fori_loop(0, slots, one, 0)

    stride = LIST + slots
    for e in range(NX):
        lists[e * stride] = 0

    def note(n, _):
        @pl.when(meta[HEAD + n] == 2)
        def _():
            at = meta[HEAD + slots + n] // (cols.shape[0] // NX) * stride
            count = lists[at] + 1
            lists[at] = count
            for u in range(LIST):
                lists[at + count + u] = n

        return 0

    lax.fori_loop(0, slots, note, 0)


def late_kernel(slots, meta, lists, cols, *refs):
    sources, refs = refs[:NX], refs[NX + 2 * CUTS :]
    keep, send, (rows, sems) = refs[:CUTS], refs[CUTS : 2 * CUTS], refs[2 * CUTS :]
    per = sources[0].shape[0]
    copies = [
        pltpu.make_async_copy(sources[e], rows.at[pl.ds(e * per, per)], sems.at[e])
        for e in range(NX)
    ]
    for copy in copies:
        copy.start()
    for e in range(NX):
        copies[e].wait()

        def some(i, _):
            ids = [lists[e * (LIST + slots) + 1 + i * TOGETHER + u] for u in range(TOGETHER)]
            made = [
                jnp.dot(
                    rows[meta[HEAD + slots + n]],
                    cols[meta[HEAD + 2 * slots + n]],
                    preferred_element_type=jnp.float32,
                )
                for n in ids
            ]
            for n, product in zip(ids, made):
                put(meta, n, product, keep, send)
            return 0

        lax.fori_loop(0, (lists[e * (LIST + slots)] + TOGETHER - 1) // TOGETHER, some, 0)


def early(meta, source, count, tokens, slots):
    width = source.shape[2]
    half = jax.ShapeDtypeStruct((slots * QUARTER // 2, width // CUTS), jnp.float32)
    return pl.pallas_call(
        functools.partial(early_kernel, slots),
        out_shape=[half] * (2 * CUTS)
        + [
            jax.ShapeDtypeStruct((count, tokens, width), jnp.bfloat16),
            jax.ShapeDtypeStruct((NX * (LIST + slots),), jnp.int32),
        ],
        in_specs=[SMEM, ANY],
        out_specs=[VMEM] * (2 * CUTS + 1) + [SMEM],
        scratch_shapes=[
            pltpu.VMEM((count, QUARTER, tokens), jnp.bfloat16),
            pltpu.SemaphoreType.DMA((count,)),
        ],
        compiler_params=pltpu.CompilerParams(vmem_limit_bytes=24 << 20),
        cost_estimate=pl.CostEstimate(flops=0, bytes_accessed=0, transcendentals=0),
    )(meta, source)


def late(meta, lists, cols, sources, halves, slots):
    per, quarter, tokens = sources[0].shape
    return pl.pallas_call(
        functools.partial(late_kernel, slots),
        out_shape=[jax.ShapeDtypeStruct(h.shape, h.dtype) for h in halves],
        in_specs=[SMEM, SMEM, VMEM] + [ANY] * NX + [VMEM] * len(halves),
        out_specs=[VMEM] * len(halves),
        scratch_shapes=[
            pltpu.VMEM((NX * per, quarter, tokens), jnp.bfloat16),
            pltpu.SemaphoreType.DMA((NX,)),
        ],
        input_output_aliases={3 + NX + i: i for i in range(len(halves))},
        compiler_params=pltpu.CompilerParams(vmem_limit_bytes=24 << 20),
    )(meta, lists, cols, *sources, *halves)


def body(activations, block_map):
    tokens, blocks, width = activations.shape
    y, zi, core = (lax.axis_index(a) for a in ("y", "zi", "core"))
    zh, x = lax.axis_index("zh"), lax.axis_index("x")

    own = jnp.transpose(activations, (1, 0, 2))
    pieces = quarters(x, own)
    low = [
        lax.ppermute(piece, ("zh", "x"), [(i, NX + (i ^ e)) for i in range(NX)])
        for e, piece in enumerate(pieces)
    ]
    rows = blocks * tokens + block_map.shape[1]
    half = lax.cond(
        block_map[0, 0, 0] >= -1,
        exchange,
        lambda own, pairs: jnp.zeros((NX, rows, width), own.dtype),
        own,
        block_map[0],
    )
    pairs = half[:, blocks * tokens :, :2].astype(jnp.int32).reshape(-1, 2)
    slots = pairs.shape[0]
    row, col = jnp.maximum(pairs[:, 0], 0), jnp.maximum(pairs[:, 1], 0)
    live, same = pairs[:, 0] >= 0, row // blocks // NX == zh
    kind = jnp.where(live, jnp.where(same, 1, 2), 0)
    row_at = jnp.where(same, row // blocks % NX, row // blocks % NX ^ x) * blocks + row % blocks
    col_at = col % (NX * blocks)
    head = jnp.stack([y, zi, core, x, zh, zh, zh, zh])
    meta = jnp.concatenate([head, kind, row_at, col_at]).astype(jnp.int32)

    *halves, cols, lists = early(meta, half, NX * blocks, tokens, slots)
    halves = late(meta, lists, cols, low, halves, slots)
    scale = 2.0 / (tokens * NY * NZ * NC)
    left, right = (keep + swap(send, "core", 1) for keep, send in zip(halves[:CUTS], halves[CUTS:]))
    left = total(left, (("y", 3), ("y", 1), ("zi", 1)))
    right = total(right, (("zi", 1),)).reshape(NY, -1, right.shape[1])
    right = jnp.sum(lax.all_to_all(right, "y", 0, 0, tiled=True), axis=0)
    parts = jnp.concatenate([left, right], axis=1).reshape(NP * NX, -1, width)
    parts = lax.all_to_all(parts, ("zp", "x"), 0, 0, tiled=True).reshape(NP, -1, width)
    return jnp.sum(parts, axis=0)[None] * scale


def total(kept, order):
    for axis, e in order:
        half = kept.shape[0] // 2
        kept = kept[:half] + swap(kept[half:], axis, e)
    return kept


def solution(mesh):
    grid = mesh.devices.reshape(NY, NP, 2, NC, NH, NX)
    tok, slab = ("y", "zp", "zi", "core"), ("zh", "x")
    return jax.shard_map(
        body,
        mesh=Mesh(grid, tok + slab),
        in_specs=(P(tok, slab, None), P(slab, None, None)),
        out_specs=P(slab, tok, None),
        check_vma=False,
    )
```

```python
import functools

import jax
import jax.numpy as jnp
from jax import lax
from jax.experimental import pallas as pl
from jax.experimental.pallas import tpu as pltpu
from jax.sharding import Mesh, PartitionSpec as P

NY, NZ, NC, NH, NX = 4, 8, 2, 2, 4
NP = NZ // 2
SIZES = {"y": NY, "zi": 2, "core": NC, "x": NX}
CUTS = 2
TOGETHER = 4
LIST = TOGETHER
QUARTER = 64
VMEM = pl.BlockSpec(memory_space=pltpu.VMEM)
SMEM = pl.BlockSpec(memory_space=pltpu.SMEM)
ANY = pl.BlockSpec(memory_space=pl.ANY)


def swap(v, axis, e):
    return lax.ppermute(v, axis, [(i, i ^ e) for i in range(SIZES[axis])])


def quarter_picker(x, width):
    p = lax.broadcasted_iota(jnp.int32, (QUARTER, width), 0)
    f = lax.broadcasted_iota(jnp.int32, (QUARTER, width), 1)
    wanted = (p // 32) * 128 + ((p // 16) % 2) * 64 + x * 16 + p % 16
    return (f == wanted).astype(jnp.float32).astype(jnp.bfloat16)


def pick(picker, block):
    return lax.dot_general(
        picker, block, (((1,), (1,)), ((), ())), preferred_element_type=jnp.float32
    ).astype(jnp.bfloat16)


def quarters_kernel(meta, own, *outs):
    for d in range(NX):
        picker = quarter_picker(meta[0] ^ d, own.shape[2])
        for b in range(own.shape[0]):
            outs[d][b] = pick(picker, own[b])


def quarters(x, own):
    blocks, tokens, width = own.shape
    return pl.pallas_call(
        quarters_kernel,
        out_shape=[jax.ShapeDtypeStruct((blocks, QUARTER, tokens), jnp.bfloat16)] * NX,
        in_specs=[SMEM, VMEM],
        out_specs=[VMEM] * NX,
        compiler_params=pltpu.CompilerParams(vmem_limit_bytes=16 << 20),
    )(x[None].astype(jnp.int32), own)


def exchange(own, pairs):
    blocks, tokens, width = own.shape
    table = jnp.pad(pairs.astype(jnp.bfloat16), ((0, 0), (0, width - pairs.shape[1])))
    load = jnp.concatenate([own.reshape(blocks * tokens, width), table])
    return lax.all_to_all(jnp.broadcast_to(load, (NX, *load.shape)), "x", 0, 0, tiled=True)


HEAD = 8


def put(meta, n, product, keep, send):
    y, zi, core = meta[0], meta[1], meta[2]
    k = lax.rem(n, 16)
    e = k // 4 ^ y
    group = e ^ (e >> 1)
    for half in range(2):
        side = half ^ zi
        starts = ((group >> 1) * 4 + side * 2 + (group & 1), side * 4 + k // 4)
        for cut in range(CUTS):
            at = ((starts[cut] * NP + lax.rem(k, 4)) * NX + n // 16) * 16
            at = pl.ds(pl.multiple_of(at, 16), 16)
            wide = keep[cut].shape[1]
            lanes = slice(cut * wide, (cut + 1) * wide)
            if product is None:
                keep[cut][at, :] = jnp.zeros((16, wide), jnp.float32)
                send[cut][at, :] = jnp.zeros((16, wide), jnp.float32)
            else:
                first = product[half * 32 : half * 32 + 16, lanes]
                second = product[half * 32 + 16 : half * 32 + 32, lanes]
                keep[cut][at, :] = jnp.where(core == 0, first, second)
                send[cut][at, :] = jnp.where(core == 0, second, first)


def early_kernel(slots, meta, source, *refs):
    keep, send, (cols, lists, rows, sems) = refs[:CUTS], refs[CUTS : 2 * CUTS], refs[2 * CUTS :]
    tokens = cols.shape[1]
    per = cols.shape[0] // NX
    copies = [
        pltpu.make_async_copy(source.at[b // per, pl.ds(b % per * tokens, tokens)], cols.at[b], sems.at[b])
        for b in range(cols.shape[0])
    ]
    for copy in copies:
        copy.start()
    picker = quarter_picker(meta[3], cols.shape[2])
    for b, copy in enumerate(copies):
        copy.wait()
        rows[b] = pick(picker, cols[b])

    def one(n, _):
        @pl.when(meta[HEAD + n] == 0)
        def _():
            put(meta, n, None, keep, send)

        @pl.when(meta[HEAD + n] == 1)
        def _():
            product = jnp.dot(
                rows[meta[HEAD + slots + n]],
                cols[meta[HEAD + 2 * slots + n]],
                preferred_element_type=jnp.float32,
            )
            put(meta, n, product, keep, send)

        return 0

    lax.fori_loop(0, slots, one, 0)

    stride = LIST + slots
    for e in range(NX):
        lists[e * stride] = 0

    def note(n, _):
        @pl.when(meta[HEAD + n] == 2)
        def _():
            at = meta[HEAD + slots + n] // (cols.shape[0] // NX) * stride
            count = lists[at] + 1
            lists[at] = count
            for u in range(LIST):
                lists[at + count + u] = n

        return 0

    lax.fori_loop(0, slots, note, 0)


def late_kernel(slots, meta, lists, cols, *refs):
    sources, refs = refs[:NX], refs[NX + 2 * CUTS :]
    keep, send, (rows, sems) = refs[:CUTS], refs[CUTS : 2 * CUTS], refs[2 * CUTS :]
    per = sources[0].shape[0]
    copies = [
        pltpu.make_async_copy(sources[e], rows.at[pl.ds(e * per, per)], sems.at[e])
        for e in range(NX)
    ]
    for copy in copies:
        copy.start()
    for e in range(NX):
        copies[e].wait()

        def some(i, _):
            ids = [lists[e * (LIST + slots) + 1 + i * TOGETHER + u] for u in range(TOGETHER)]
            made = [
                jnp.dot(
                    rows[meta[HEAD + slots + n]],
                    cols[meta[HEAD + 2 * slots + n]],
                    preferred_element_type=jnp.float32,
                )
                for n in ids
            ]
            for n, product in zip(ids, made):
                put(meta, n, product, keep, send)
            return 0

        lax.fori_loop(0, (lists[e * (LIST + slots)] + TOGETHER - 1) // TOGETHER, some, 0)


def early(meta, source, count, tokens, slots):
    width = source.shape[2]
    half = jax.ShapeDtypeStruct((slots * QUARTER // 2, width // CUTS), jnp.float32)
    return pl.pallas_call(
        functools.partial(early_kernel, slots),
        out_shape=[half] * (2 * CUTS)
        + [
            jax.ShapeDtypeStruct((count, tokens, width), jnp.bfloat16),
            jax.ShapeDtypeStruct((NX * (LIST + slots),), jnp.int32),
        ],
        in_specs=[SMEM, ANY],
        out_specs=[VMEM] * (2 * CUTS + 1) + [SMEM],
        scratch_shapes=[
            pltpu.VMEM((count, QUARTER, tokens), jnp.bfloat16),
            pltpu.SemaphoreType.DMA((count,)),
        ],
        compiler_params=pltpu.CompilerParams(vmem_limit_bytes=24 << 20),
        cost_estimate=pl.CostEstimate(flops=0, bytes_accessed=0, transcendentals=0),
    )(meta, source)


def late(meta, lists, cols, sources, halves, slots):
    per, quarter, tokens = sources[0].shape
    return pl.pallas_call(
        functools.partial(late_kernel, slots),
        out_shape=[jax.ShapeDtypeStruct(h.shape, h.dtype) for h in halves],
        in_specs=[SMEM, SMEM, VMEM] + [ANY] * NX + [VMEM] * len(halves),
        out_specs=[VMEM] * len(halves),
        scratch_shapes=[
            pltpu.VMEM((NX * per, quarter, tokens), jnp.bfloat16),
            pltpu.SemaphoreType.DMA((NX,)),
        ],
        input_output_aliases={3 + NX + i: i for i in range(len(halves))},
        compiler_params=pltpu.CompilerParams(vmem_limit_bytes=24 << 20),
    )(meta, lists, cols, *sources, *halves)


def body(activations, block_map):
    tokens, blocks, width = activations.shape
    y, zi, core = (lax.axis_index(a) for a in ("y", "zi", "core"))
    zh, x = lax.axis_index("zh"), lax.axis_index("x")

    own = jnp.transpose(activations, (1, 0, 2))
    pieces = quarters(x, own)
    low = [
        lax.ppermute(piece, ("zh", "x"), [(i, NX + (i ^ e)) for i in range(NX)])
        for e, piece in enumerate(pieces)
    ]
    rows = blocks * tokens + block_map.shape[1]
    half = lax.cond(
        block_map[0, 0, 0] >= -1,
        exchange,
        lambda own, pairs: jnp.zeros((NX, rows, width), own.dtype),
        own,
        block_map[0],
    )
    pairs = half[:, blocks * tokens :, :2].astype(jnp.int32).reshape(-1, 2)
    slots = pairs.shape[0]
    row, col = jnp.maximum(pairs[:, 0], 0), jnp.maximum(pairs[:, 1], 0)
    live, same = pairs[:, 0] >= 0, row // blocks // NX == zh
    kind = jnp.where(live, jnp.where(same, 1, 2), 0)
    row_at = jnp.where(same, row // blocks % NX, row // blocks % NX ^ x) * blocks + row % blocks
    col_at = col % (NX * blocks)
    head = jnp.stack([y, zi, core, x, zh, zh, zh, zh])
    meta = jnp.concatenate([head, kind, row_at, col_at]).astype(jnp.int32)

    *halves, cols, lists = early(meta, half, NX * blocks, tokens, slots)
    halves = late(meta, lists, cols, low, halves, slots)
    scale = 2.0 / (tokens * NY * NZ * NC)
    left, right = (keep + swap(send, "core", 1) for keep, send in zip(halves[:CUTS], halves[CUTS:]))
    left = total(left, (("y", 3), ("zi", 1), ("y", 1)))
    right = total(right, (("zi", 1),)).reshape(NY, -1, right.shape[1])
    right = jnp.sum(lax.all_to_all(right, "y", 0, 0, tiled=True), axis=0)
    parts = jnp.concatenate([left, right], axis=1).reshape(NP * NX, -1, width)
    parts = lax.all_to_all(parts, ("zp", "x"), 0, 0, tiled=True).reshape(NP, -1, width)
    return jnp.sum(parts, axis=0)[None] * scale


def total(kept, order):
    for axis, e in order:
        half = kept.shape[0] // 2
        kept = kept[:half] + swap(kept[half:], axis, e)
    return kept


def solution(mesh):
    grid = mesh.devices.reshape(NY, NP, 2, NC, NH, NX)
    tok, slab = ("y", "zp", "zi", "core"), ("zh", "x")
    return jax.shard_map(
        body,
        mesh=Mesh(grid, tok + slab),
        in_specs=(P(tok, slab, None), P(slab, None, None)),
        out_specs=P(slab, tok, None),
        check_vma=False,
    )
```

```python
import functools

import jax
import jax.numpy as jnp
from jax import lax
from jax.experimental import pallas as pl
from jax.experimental.pallas import tpu as pltpu
from jax.sharding import Mesh, PartitionSpec as P

NY, NZ, NC, NH, NX = 4, 8, 2, 2, 4
NP = NZ // 2
SIZES = {"y": NY, "zi": 2, "core": NC, "x": NX}
CUTS = 2
TOGETHER = 4
LIST = TOGETHER
QUARTER = 64
VMEM = pl.BlockSpec(memory_space=pltpu.VMEM)
SMEM = pl.BlockSpec(memory_space=pltpu.SMEM)
ANY = pl.BlockSpec(memory_space=pl.ANY)


def swap(v, axis, e):
    return lax.ppermute(v, axis, [(i, i ^ e) for i in range(SIZES[axis])])


def quarter_picker(x, width):
    p = lax.broadcasted_iota(jnp.int32, (QUARTER, width), 0)
    f = lax.broadcasted_iota(jnp.int32, (QUARTER, width), 1)
    wanted = (p // 32) * 128 + ((p // 16) % 2) * 64 + x * 16 + p % 16
    return (f == wanted).astype(jnp.float32).astype(jnp.bfloat16)


def pick(picker, block):
    return lax.dot_general(
        picker, block, (((1,), (1,)), ((), ())), preferred_element_type=jnp.float32
    ).astype(jnp.bfloat16)


def quarters_kernel(places, meta, own, *outs):
    for d, out in zip(places, outs):
        picker = quarter_picker(meta[0] ^ d, own.shape[2])
        for b in range(own.shape[0]):
            out[b] = pick(picker, own[b])


def quarters(x, own, places):
    blocks, tokens, width = own.shape
    return pl.pallas_call(
        functools.partial(quarters_kernel, places),
        out_shape=[jax.ShapeDtypeStruct((blocks, QUARTER, tokens), jnp.bfloat16)] * len(places),
        in_specs=[SMEM, VMEM],
        out_specs=[VMEM] * len(places),
        compiler_params=pltpu.CompilerParams(vmem_limit_bytes=16 << 20),
    )(x[None].astype(jnp.int32), own)


def exchange(own, pairs):
    blocks, tokens, width = own.shape
    table = jnp.pad(pairs.astype(jnp.bfloat16), ((0, 0), (0, width - pairs.shape[1])))
    load = jnp.concatenate([own.reshape(blocks * tokens, width), table])
    return lax.all_to_all(jnp.broadcast_to(load, (NX, *load.shape)), "x", 0, 0, tiled=True)


HEAD = 8


def put(meta, n, product, keep, send):
    y, zi, core = meta[0], meta[1], meta[2]
    k = lax.rem(n, 16)
    e = k // 4 ^ y
    group = e ^ (e >> 1)
    for half in range(2):
        side = half ^ zi
        starts = (group * 2 + side, side * 4 + k // 4)
        for cut in range(CUTS):
            at = ((starts[cut] * NP + lax.rem(k, 4)) * NX + n // 16) * 16
            at = pl.ds(pl.multiple_of(at, 16), 16)
            wide = keep[cut].shape[1]
            lanes = slice(cut * wide, (cut + 1) * wide)
            if product is None:
                keep[cut][at, :] = jnp.zeros((16, wide), jnp.float32)
                send[cut][at, :] = jnp.zeros((16, wide), jnp.float32)
            else:
                first = product[half * 32 : half * 32 + 16, lanes]
                second = product[half * 32 + 16 : half * 32 + 32, lanes]
                keep[cut][at, :] = jnp.where(core == 0, first, second)
                send[cut][at, :] = jnp.where(core == 0, second, first)


def early_kernel(slots, meta, source, *refs):
    keep, send, (cols, lists, rows, sems) = refs[:CUTS], refs[CUTS : 2 * CUTS], refs[2 * CUTS :]
    tokens = cols.shape[1]
    per = cols.shape[0] // NX
    copies = [
        pltpu.make_async_copy(source.at[b // per, pl.ds(b % per * tokens, tokens)], cols.at[b], sems.at[b])
        for b in range(cols.shape[0])
    ]
    for copy in copies:
        copy.start()
    picker = quarter_picker(meta[3], cols.shape[2])
    for b, copy in enumerate(copies):
        copy.wait()
        rows[b] = pick(picker, cols[b])

    def one(n, _):
        @pl.when(meta[HEAD + n] == 0)
        def _():
            put(meta, n, None, keep, send)

        @pl.when(meta[HEAD + n] == 1)
        def _():
            product = jnp.dot(
                rows[meta[HEAD + slots + n]],
                cols[meta[HEAD + 2 * slots + n]],
                preferred_element_type=jnp.float32,
            )
            put(meta, n, product, keep, send)

        return 0

    lax.fori_loop(0, slots, one, 0)

    stride = LIST + slots
    for e in range(NX):
        lists[e * stride] = 0

    def note(n, _):
        @pl.when(meta[HEAD + n] == 2)
        def _():
            at = meta[HEAD + slots + n] // (cols.shape[0] // NX) * stride
            count = lists[at] + 1
            lists[at] = count
            for u in range(LIST):
                lists[at + count + u] = n

        return 0

    lax.fori_loop(0, slots, note, 0)


def late_kernel(slots, meta, lists, cols, *refs):
    sources, refs = refs[:NX], refs[NX + 2 * CUTS :]
    keep, send, (rows, sems) = refs[:CUTS], refs[CUTS : 2 * CUTS], refs[2 * CUTS :]
    per = sources[0].shape[0]
    copies = [
        pltpu.make_async_copy(sources[e], rows.at[pl.ds(e * per, per)], sems.at[e])
        for e in range(NX)
    ]
    for copy in copies:
        copy.start()
    for e in range(NX):
        copies[e].wait()

        def some(i, _):
            ids = [lists[e * (LIST + slots) + 1 + i * TOGETHER + u] for u in range(TOGETHER)]
            made = [
                jnp.dot(
                    rows[meta[HEAD + slots + n]],
                    cols[meta[HEAD + 2 * slots + n]],
                    preferred_element_type=jnp.float32,
                )
                for n in ids
            ]
            for n, product in zip(ids, made):
                put(meta, n, product, keep, send)
            return 0

        lax.fori_loop(0, (lists[e * (LIST + slots)] + TOGETHER - 1) // TOGETHER, some, 0)


def early(meta, source, count, tokens, slots):
    width = source.shape[2]
    half = jax.ShapeDtypeStruct((slots * QUARTER // 2, width // CUTS), jnp.float32)
    return pl.pallas_call(
        functools.partial(early_kernel, slots),
        out_shape=[half] * (2 * CUTS)
        + [
            jax.ShapeDtypeStruct((count, tokens, width), jnp.bfloat16),
            jax.ShapeDtypeStruct((NX * (LIST + slots),), jnp.int32),
        ],
        in_specs=[SMEM, ANY],
        out_specs=[VMEM] * (2 * CUTS + 1) + [SMEM],
        scratch_shapes=[
            pltpu.VMEM((count, QUARTER, tokens), jnp.bfloat16),
            pltpu.SemaphoreType.DMA((count,)),
        ],
        compiler_params=pltpu.CompilerParams(vmem_limit_bytes=24 << 20),
        cost_estimate=pl.CostEstimate(flops=0, bytes_accessed=0, transcendentals=0),
    )(meta, source)


def late(meta, lists, cols, sources, halves, slots):
    per, quarter, tokens = sources[0].shape
    return pl.pallas_call(
        functools.partial(late_kernel, slots),
        out_shape=[jax.ShapeDtypeStruct(h.shape, h.dtype) for h in halves],
        in_specs=[SMEM, SMEM, VMEM] + [ANY] * NX + [VMEM] * len(halves),
        out_specs=[VMEM] * len(halves),
        scratch_shapes=[
            pltpu.VMEM((NX * per, quarter, tokens), jnp.bfloat16),
            pltpu.SemaphoreType.DMA((NX,)),
        ],
        input_output_aliases={3 + NX + i: i for i in range(len(halves))},
        compiler_params=pltpu.CompilerParams(vmem_limit_bytes=24 << 20),
    )(meta, lists, cols, *sources, *halves)


def body(activations, block_map):
    tokens, blocks, width = activations.shape
    y, zi, core = (lax.axis_index(a) for a in ("y", "zi", "core"))
    zh, x = lax.axis_index("zh"), lax.axis_index("x")

    own = jnp.transpose(activations, (1, 0, 2))
    pieces = [*quarters(x, own, (0,)), *quarters(x, own, (1, 2, 3))]
    low = [
        lax.ppermute(piece, ("zh", "x"), [(i, NX + (i ^ e)) for i in range(NX)])
        for e, piece in enumerate(pieces)
    ]
    rows = blocks * tokens + block_map.shape[1]
    half = lax.cond(
        block_map[0, 0, 0] >= -1,
        exchange,
        lambda own, pairs: jnp.zeros((NX, rows, width), own.dtype),
        own,
        block_map[0],
    )
    pairs = half[:, blocks * tokens :, :2].astype(jnp.int32).reshape(-1, 2)
    slots = pairs.shape[0]
    row, col = jnp.maximum(pairs[:, 0], 0), jnp.maximum(pairs[:, 1], 0)
    live, same = pairs[:, 0] >= 0, row // blocks // NX == zh
    kind = jnp.where(live, jnp.where(same, 1, 2), 0)
    row_at = jnp.where(same, row // blocks % NX, row // blocks % NX ^ x) * blocks + row % blocks
    col_at = col % (NX * blocks)
    head = jnp.stack([y, zi, core, x, zh, zh, zh, zh])
    meta = jnp.concatenate([head, kind, row_at, col_at]).astype(jnp.int32)

    *halves, cols, lists = early(meta, half, NX * blocks, tokens, slots)
    halves = late(meta, lists, cols, low, halves, slots)
    scale = 2.0 / (tokens * NY * NZ * NC)
    left, right = (keep + swap(send, "core", 1) for keep, send in zip(halves[:CUTS], halves[CUTS:]))
    left = total(left, (("y", 3), ("y", 1), ("zi", 1)))
    right = total(right, (("zi", 1),)).reshape(NY, -1, right.shape[1])
    right = jnp.sum(lax.all_to_all(right, "y", 0, 0, tiled=True), axis=0)
    parts = jnp.concatenate([left, right], axis=1).reshape(NP * NX, -1, width)
    parts = lax.all_to_all(parts, ("zp", "x"), 0, 0, tiled=True).reshape(NP, -1, width)
    return jnp.sum(parts, axis=0)[None] * scale


def total(kept, order):
    for axis, e in order:
        half = kept.shape[0] // 2
        kept = kept[:half] + swap(kept[half:], axis, e)
    return kept


def solution(mesh):
    grid = mesh.devices.reshape(NY, NP, 2, NC, NH, NX)
    tok, slab = ("y", "zp", "zi", "core"), ("zh", "x")
    return jax.shard_map(
        body,
        mesh=Mesh(grid, tok + slab),
        in_specs=(P(tok, slab, None), P(slab, None, None)),
        out_specs=P(slab, tok, None),
        check_vma=False,
    )
```
